32 devices in a mesh: row: 8 (over z, core), col: 2 (over y), pair: 2 (over x).
Axes of the slice: x: 2, y: 2, z: 4, core: 2. Of those that a mesh axis runs over, the one named last changes fastest.
Arguments:
- amplitudes: bfloat16 [320, 8, 320], P('row', 'pair', 'col'), may hold values from -6 to 6
- factors: bfloat16 [2048, 320, 320], P(('row', 'col', 'pair')), may hold values from -0.078125 to 0.078125
- vir_irrep: int32 [320], replicated, may hold values from 0 to 7, never falling along the last dimension, each value on 1 to 80 neighbouring positions
- pair_irrep: int32 [8], P('pair'), may hold values from 0 to 7
Outputs:
- ladder_term: float32 [320, 8, 320], P('row', 'pair', 'col')
The draws below stay inside these ranges and needn't reach their ends.
Inputs may be any that keep to these rules, and one draw needn't show every extreme that they name: `vir_irrep`: labels never fall along the virtual index, so each label holds one contiguous block of virtuals.
All inputs are finite; a program needn't handle non-finite values.
Results may differ from the reference program's by a relative error of at most 0.0025.
Values may be sent and summed in bfloat16 or wider, within the bound.
A program may use at most 128 MiB of HBM per device.

```python
import math
import jax
import jax.numpy as jnp
import numpy as np
from jax import lax

V = 320
NQ = 2048
PAIRS = 8


def touch_ends(result, rng, low, largest):
    place = [jax.random.randint(jax.random.fold_in(rng, axis), (), 0, length) for axis, length in enumerate(result.shape)]
    main_axis = result.shape.index(max(result.shape))
    beside = place[:main_axis] + [(place[main_axis] + 1) % result.shape[main_axis]] + place[main_axis + 1:]
    return result.at[tuple(place)].set(low).at[tuple(beside)].set(largest)


def raised(array, own_key, source, target, parts, factor):
    owner, partner = [(jnp.arange(array.shape[axis_at]) // (array.shape[axis_at] // parts)).reshape([-1 if axis == axis_at else 1 for axis in range(array.ndim)]) for axis_at in (source, target)]
    chosen = jax.random.permutation(own_key, parts)[partner]
    strong = (owner == chosen) | (owner == (partner + parts // 2) % parts)
    return jnp.where(strong, factor * array, array)


def block_scale(rng, shape, shards, low, largest):
    def one(dim, parts):
        steps = jax.random.uniform(jax.random.fold_in(jax.random.fold_in(rng, 6), dim), (parts,), jnp.float32, low / len(shards), largest / len(shards))
        return jnp.repeat(jnp.exp(steps), shape[dim] // parts).reshape((-1,) + (1,) * (len(shape) - dim - 1))

    level = one(*shards[0])
    for cut in shards[1:]:
        level = level * one(*cut)
    return level


def length_profile(count, total, limit, skew):
    weights = [(1 << 20) // math.isqrt(standing ** skew) + 1 for standing in range(2, count + 1)]
    surplus, given = total - limit - (count - 1), [1] * (count - 1)
    while surplus > 0:
        movable = [i for i in range(count - 1) if given[i] < limit]
        pool, remaining = sum([weights[i] for i in movable]), surplus
        for i in movable:
            addition = min(limit - given[i], max(1, remaining * weights[i] // pool), surplus)
            given[i] = given[i] + addition
            surplus = surplus - addition
    return np.array([limit] + given)


def ragged_sizes(key, amount, total, limit, skew):
    if amount == 2:
        one = jax.random.randint(key, (), max(1, total - limit), min(limit, total - 1) + 1)
        return jnp.stack([one, total - one])
    tallies = jnp.asarray(length_profile(amount, total, limit, skew), jnp.int32)
    couples = (amount - 1) // 2
    donor, taker = tallies[1:1 + 2 * couples:2], tallies[2:2 + 2 * couples:2]
    slack = jnp.minimum(donor - 1, limit - taker)
    shifted = jax.random.randint(jax.random.fold_in(key, 1), (couples,), 0, 1 << 20) % (slack + 1)
    tallies = tallies.at[1:1 + 2 * couples:2].set(donor - shifted).at[2:2 + 2 * couples:2].set(taker + shifted)
    return tallies[jax.random.permutation(jax.random.fold_in(key, 2), amount)]


def noise(rng, shape, scale, most, shards=(), dtype=jnp.bfloat16):
    loudness = block_scale(rng, shape, shards, -0.22, 0.18) if shards else 1.0
    values = jax.random.normal(rng, shape, jnp.float32) * scale * loudness
    return jnp.minimum(jnp.maximum(values, -most), most).astype(dtype)


def gaussian_with(stream_key, extent, spread, most, pieces, heavy, dtype=jnp.bfloat16):
    values = spread * jax.random.normal(stream_key, extent, jnp.float32)
    if pieces:
        values = values * block_scale(stream_key, extent, pieces, -0.22, 0.18)
    return jnp.clip(raised(values, jax.random.fold_in(stream_key, 3), *heavy), -most, most).astype(dtype)


def setup_inputs(seed: int = 0) -> dict:
    key_of = jax.random.split(jax.random.key(seed), 5)
    amplitudes = noise(key_of[0], (V, PAIRS, V), 1.0, 6.0, ((0, 8), (1, 2), (2, 2)))
    factors = gaussian_with(key_of[1], (NQ, V, V), (64 * V) ** -0.5, 0.078125, ((0, 32),), (0, 1, 32, 2.75))
    vir_irrep = jnp.searchsorted(jnp.cumsum(ragged_sizes(key_of[2], 8, V, V // 4, 1)), jnp.arange(V), side="right").astype(jnp.int32)
    pair_irrep = touch_ends(jax.random.randint(key_of[3], (PAIRS,), 0, 8), jax.random.fold_in(key_of[3], 1), 0, 7).astype(jnp.int32)
    return {"amplitudes": amplitudes, "factors": factors, "vir_irrep": vir_irrep, "pair_irrep": pair_irrep}


def reference(amplitudes, factors, vir_irrep, pair_irrep):
    pair_count = amplitudes.shape[1]
    mixed = jnp.bitwise_xor(vir_irrep[:, None, None], vir_irrep[None, None, :])
    allowed = mixed == pair_irrep[None, :, None]
    sym_amp = jnp.where(allowed, amplitudes, jnp.zeros_like(amplitudes))
    amp_matrix = sym_amp.reshape(V, pair_count * V)

    def one_factor(summed, factor):
        inner = jnp.dot(factor, amp_matrix, preferred_element_type=jnp.float32).astype(jnp.bfloat16)
        inner = inner.reshape(V * pair_count, V)
        outer = jnp.dot(inner, factor.T, preferred_element_type=jnp.float32)
        return summed + outer.reshape(V, pair_count, V), None

    start = jnp.zeros((V, pair_count, V), jnp.float32)
    ladder = lax.scan(one_factor, start, factors)[0]
    both = ladder + jnp.transpose(ladder, (2, 1, 0))
    return jnp.where(allowed, both, jnp.zeros_like(both))
```

```python
import functools

import jax
import jax.numpy as jnp
from jax import lax
from jax.experimental import pallas as pl
from jax.experimental.pallas import tpu as pltpu
from jax.sharding import PartitionSpec as P

LANES = 128
GROUPS = 1
AXES = ("row", "col", "pair")


def ladder_kernel(pairs, padded, f_ref, t_ref, o_ref, f_scr, x_scr):
    batch, width, _ = f_ref.shape

    @pl.when(pl.program_id(0) == 0)
    def _():
        o_ref[...] = jnp.zeros_like(o_ref)
        f_scr[...] = jnp.zeros_like(f_scr)

    for q in range(batch):
        f_scr[:, q * padded : q * padded + width] = f_ref[q]
    for p in range(pairs):
        for q in range(batch):
            x_scr[p, :, q * padded : (q + 1) * padded] = jnp.dot(
                f_ref[q], t_ref[:, p * padded : (p + 1) * padded],
                preferred_element_type=jnp.float32,
            ).astype(jnp.bfloat16)
        o_ref[p] += lax.dot_general(
            x_scr[p], f_scr[...], (((1,), (1,)), ((), ())),
            preferred_element_type=jnp.float32,
        )


def partial_ladder(factors, t, pairs, padded):
    aux, width, _ = factors.shape
    batch = 4 if aux % 4 == 0 else 1
    return pl.pallas_call(
        functools.partial(ladder_kernel, pairs, padded),
        grid=(aux // batch,),
        in_specs=[
            pl.BlockSpec((batch, width, width), lambda i: (i, 0, 0)),
            pl.BlockSpec((width, pairs * padded), lambda i: (0, 0)),
        ],
        out_specs=pl.BlockSpec((pairs, width, width), lambda i: (0, 0, 0)),
        out_shape=jax.ShapeDtypeStruct((pairs, width, width), jnp.float32),
        scratch_shapes=[
            pltpu.VMEM((width, batch * padded), jnp.bfloat16),
            pltpu.VMEM((pairs, width, batch * padded), jnp.bfloat16),
        ],
        compiler_params=pltpu.CompilerParams(vmem_limit_bytes=56 * 1024 * 1024),
        cost_estimate=pl.CostEstimate(
            flops=4 * aux * width * width * width * pairs,
            bytes_accessed=2 * aux * width * width,
            transcendentals=0,
        ),
    )(factors, t)


def body(mesh_shape, amplitudes, factors, vir_irrep, pair_irrep):
    rows, cols, pgroups = (mesh_shape[name] for name in AXES)
    row_block, pairs_here, col_block = amplitudes.shape
    width = factors.shape[1]
    limit = width // 4
    padded = -(-width // LANES) * LANES
    row_labels = lax.dynamic_slice_in_dim(vir_irrep, lax.axis_index("row") * row_block, row_block)
    col_labels = lax.dynamic_slice_in_dim(vir_irrep, lax.axis_index("col") * col_block, col_block)
    mixed = jnp.bitwise_xor(row_labels[:, None, None], col_labels[None, None, :])
    allowed = mixed == pair_irrep[None, :, None]
    sym_amp = jnp.where(allowed, amplitudes, jnp.zeros_like(amplitudes))
    if col_block % limit == 0:
        folded = jnp.sum(
            sym_amp.reshape(row_block, pairs_here, col_block // limit, limit), axis=2,
            dtype=jnp.float32).astype(jnp.bfloat16)
    else:
        folded = sym_amp
    piece = folded.shape[2]
    all_pairs = lax.all_gather(pair_irrep, "pair", axis=0)
    vir_mixed = jnp.bitwise_xor(vir_irrep[:, None], vir_irrep[None, :])
    own = pairs_here // GROUPS
    results = []
    for g in range(GROUPS):
        sent = folded[:, g * own : (g + 1) * own]
        got = lax.all_gather(sent.reshape(-1), AXES, axis=0)
        got = got.reshape(rows, cols, pgroups, row_block, own, piece)
        got = jnp.transpose(got, (0, 3, 2, 4, 1, 5))
        got = got.reshape(width, pgroups * own, cols, 1, piece)
        got = jnp.broadcast_to(got, (width, pgroups * own, cols, col_block // piece, piece))
        got = got.reshape(width, pgroups * own, width)
        pis = all_pairs[:, g * own : (g + 1) * own].reshape(-1)
        keep = vir_mixed[:, None, :] == pis[None, :, None]
        t = jnp.where(keep, got, jnp.zeros_like(got))
        t = jnp.pad(t, ((0, 0), (0, 0), (0, padded - width)))
        t = t.reshape(width, pgroups * own * padded)
        part = partial_ladder(factors, t, pgroups * own, padded)
        both = part + jnp.swapaxes(part, 1, 2)
        both = jnp.where(vir_mixed[None] == pis[:, None, None], both, jnp.zeros_like(both))
        packed = jnp.sum(both.reshape(pgroups * own, width, width // limit, limit), axis=2)
        packed = packed.reshape(pgroups, own, rows, row_block, cols, limit // cols)
        packed = jnp.transpose(packed, (2, 4, 0, 3, 1, 5))
        packed = packed.reshape(rows * cols * pgroups, -1)
        mine = lax.psum_scatter(packed, AXES, scatter_dimension=0, tiled=False)
        mine = lax.all_gather(mine, "col", axis=0)
        mine = mine.reshape(cols, row_block, own, limit // cols)
        results.append(jnp.transpose(mine, (1, 2, 0, 3)).reshape(row_block, own, limit))
    mine = jnp.concatenate(results, axis=1)
    spread = jnp.tile(mine, (1, 1, width // limit))
    spread = lax.dynamic_slice_in_dim(spread, lax.axis_index("col") * col_block, col_block, axis=2)
    return jnp.where(allowed, spread, jnp.zeros_like(spread))


def solution(mesh):
    placed = (P("row", "pair", "col"), P(("row", "col", "pair"), None, None), P(), P("pair"))
    return jax.shard_map(
        functools.partial(body, dict(mesh.shape)), mesh=mesh, in_specs=placed,
        out_specs=P("row", "pair", "col"), check_vma=False,
    )
```

```python
import functools

import jax
import jax.numpy as jnp
from jax import lax
from jax.experimental import pallas as pl
from jax.experimental.pallas import tpu as pltpu
from jax.sharding import PartitionSpec as P

LANES = 128
AXES = ("row", "col", "pair")
MESH = pl.DeviceIdType.MESH


def place(sizes, flat):
    _, cols, pgroups = sizes
    return (flat // (cols * pgroups), (flat // pgroups) % cols, flat % pgroups)


def flat_index(sizes):
    _, cols, pgroups = sizes
    return (lax.axis_index("row") * cols + lax.axis_index("col")) * pgroups + lax.axis_index("pair")


def greet_all(sizes, me, count):
    barrier = pltpu.get_barrier_semaphore()

    def greet(k, _):
        pl.semaphore_signal(
            barrier, inc=1, device_id=place(sizes, (me + k) % count), device_id_type=MESH)
        return 0

    lax.fori_loop(1, count, greet, 0)
    pl.semaphore_wait(barrier, count - 1)


def gather_kernel(sizes, count, src_ref, out_ref, send_sem, recv_sem, own_sem):
    me = flat_index(sizes)
    greet_all(sizes, me, count)

    def copy(k):
        return pltpu.make_async_remote_copy(
            src_ref=src_ref, dst_ref=out_ref.at[me], send_sem=send_sem.at[k],
            recv_sem=recv_sem.at[k], device_id=place(sizes, (me + k) % count),
            device_id_type=MESH)

    def start(k, _):
        copy(k).start()
        return 0

    def finish(k, _):
        copy(k).wait()
        return 0

    lax.fori_loop(1, count, start, 0)
    own = pltpu.make_async_copy(src_ref, out_ref.at[me], own_sem)
    own.start()
    own.wait()
    lax.fori_loop(1, count, finish, 0)


def gather_all(sizes, count, payload):
    vmem = pl.BlockSpec(memory_space=pltpu.VMEM)
    return pl.pallas_call(
        functools.partial(gather_kernel, sizes, count),
        in_specs=[vmem], out_specs=vmem,
        out_shape=jax.ShapeDtypeStruct((count,) + payload.shape, payload.dtype),
        scratch_shapes=[
            pltpu.SemaphoreType.DMA((count,)), pltpu.SemaphoreType.DMA((count,)),
            pltpu.SemaphoreType.DMA,
        ],
        compiler_params=pltpu.CompilerParams(
            collective_id=0, has_side_effects=True, vmem_limit_bytes=32 * 1024 * 1024),
    )(payload)


def reduce_kernel(sizes, count, share, split, src_ref, out_ref, held, total, send_sem, recv_sem,
                  send_two, recv_two, own_sem):
    _, cols, pgroups = sizes
    me = flat_index(sizes)
    row, col, pair = place(sizes, me)
    pairs_here = src_ref.shape[0] // pgroups
    greet_all(sizes, me, count)

    def chunk(r, c, g):
        first = g * pairs_here + (c * share if split else 0)
        return src_ref.at[pl.ds(first, share), r]

    def copy(k):
        r, c, g = place(sizes, (me + k) % count)
        return pltpu.make_async_remote_copy(
            src_ref=chunk(r, c, g), dst_ref=held.at[k], send_sem=send_sem.at[k],
            recv_sem=recv_sem.at[k], device_id=(r, c, g), device_id_type=MESH)

    def start(k, _):
        copy(k).start()
        return 0

    lax.fori_loop(1, count, start, 0)
    own = pltpu.make_async_copy(chunk(row, col, pair), held.at[0], own_sem)
    own.start()
    own.wait()
    total[...] = held[0]

    def finish(k, _):
        copy(k).wait()
        total[...] += held[k]
        return 0

    lax.fori_loop(1, count, finish, 0)
    if not split:
        out_ref[0] = total[...]
        return
    out_ref[col] = total[...]

    def second(k):
        return pltpu.make_async_remote_copy(
            src_ref=total, dst_ref=out_ref.at[col], send_sem=send_two.at[k],
            recv_sem=recv_two.at[k], device_id=(row, (col + k) % cols, pair),
            device_id_type=MESH)

    for k in range(1, cols):
        second(k).start()
    for k in range(1, cols):
        second(k).wait()


def reduce_all(sizes, count, packed):
    _, cols, pgroups = sizes
    pairs_here = packed.shape[0] // pgroups
    split = cols > 1 and pairs_here % cols == 0
    share = pairs_here // cols if split else pairs_here
    block = (share,) + packed.shape[2:]
    vmem = pl.BlockSpec(memory_space=pltpu.VMEM)
    out = pl.pallas_call(
        functools.partial(reduce_kernel, sizes, count, share, split),
        in_specs=[vmem], out_specs=vmem,
        out_shape=jax.ShapeDtypeStruct((cols if split else 1,) + block, jnp.float32),
        scratch_shapes=[
            pltpu.VMEM((count,) + block, jnp.float32), pltpu.VMEM(block, jnp.float32),
            pltpu.SemaphoreType.DMA((count,)), pltpu.SemaphoreType.DMA((count,)),
            pltpu.SemaphoreType.DMA((cols,)), pltpu.SemaphoreType.DMA((cols,)),
            pltpu.SemaphoreType.DMA,
        ],
        compiler_params=pltpu.CompilerParams(
            collective_id=1, has_side_effects=True, vmem_limit_bytes=40 * 1024 * 1024),
    )(packed)
    return out.reshape((pairs_here,) + packed.shape[2:])


def ladder_kernel(pairs, padded, pi_ref, down_ref, across_ref, f_ref, t_ref, o_ref,
                  f_scr, x_scr, sum_scr, whole_scr):
    batch, width, _ = f_ref.shape

    @pl.when(pl.program_id(0) == 0)
    def _():
        sum_scr[...] = jnp.zeros_like(sum_scr)
        f_scr[...] = jnp.zeros_like(f_scr)
        whole_scr[...] = jnp.zeros_like(whole_scr)

    for q in range(batch):
        f_scr[:, q * padded : q * padded + width] = f_ref[q]
    side = 2 if pairs % 2 == 0 else 1
    for p in range(0, pairs, side):
        for q in range(batch):
            x = jnp.dot(
                f_ref[q], t_ref[:, p * padded : (p + side) * padded],
                preferred_element_type=jnp.float32,
            ).astype(jnp.bfloat16)
            for k in range(side):
                x_scr[
                    (p + k) * width : (p + k + 1) * width, q * padded : (q + 1) * padded
                ] = x[:, k * padded : (k + 1) * padded]
    step = 2 * LANES
    for start in range(0, pairs * width, step):
        sum_scr[:, start : start + step] += lax.dot_general(
            f_scr[...], x_scr[start : start + step], (((1,), (1,)), ((), ())),
            preferred_element_type=jnp.float32,
        )

    @pl.when(pl.program_id(0) == pl.num_programs(0) - 1)
    def _():
        mixed = jnp.bitwise_xor(down_ref[:, :1], across_ref[:1, :])

        for p in range(pairs):
            value = sum_scr[:, p * width : (p + 1) * width]
            both = jnp.where(mixed == pi_ref[p], value + value.T, 0.0)
            whole_scr[:, :width] = both
            packed = whole_scr[:, :LANES]
            for start in range(LANES, padded, LANES):
                packed = packed + whole_scr[:, start : start + LANES]
            o_ref[p] = packed


def partial_ladder(factors, t, pis, labels, padded):
    aux, width, _ = factors.shape
    pairs = pis.shape[0]
    batch = 4 if aux % 4 == 0 else 1
    down = jnp.broadcast_to(labels[:, None], (width, LANES))
    across = jnp.broadcast_to(labels[None, :], (8, width))
    return pl.pallas_call(
        functools.partial(ladder_kernel, pairs, padded),
        grid=(aux // batch,),
        in_specs=[
            pl.BlockSpec(memory_space=pltpu.SMEM),
            pl.BlockSpec((width, LANES), lambda i: (0, 0)),
            pl.BlockSpec((8, width), lambda i: (0, 0)),
            pl.BlockSpec((batch, width, width), lambda i: (i, 0, 0)),
            pl.BlockSpec((width, pairs * padded), lambda i: (0, 0)),
        ],
        out_specs=pl.BlockSpec((pairs, width, LANES), lambda i: (0, 0, 0)),
        out_shape=jax.ShapeDtypeStruct((pairs, width, LANES), jnp.float32),
        scratch_shapes=[
            pltpu.VMEM((width, batch * padded), jnp.bfloat16),
            pltpu.VMEM((pairs * width, batch * padded), jnp.bfloat16),
            pltpu.VMEM((width, pairs * width), jnp.float32),
            pltpu.VMEM((width, padded), jnp.float32),
        ],
        compiler_params=pltpu.CompilerParams(vmem_limit_bytes=56 * 1024 * 1024),
        cost_estimate=pl.CostEstimate(
            flops=4 * aux * width * width * width * pairs,
            bytes_accessed=2 * aux * width * width,
            transcendentals=0,
        ),
    )(pis, down, across, factors, t)


def body(mesh_shape, amplitudes, factors, vir_irrep, pair_irrep):
    sizes = tuple(mesh_shape[name] for name in AXES)
    rows, cols, pgroups = sizes
    count = rows * cols * pgroups
    row_block, pairs_here, col_block = amplitudes.shape
    width = factors.shape[1]
    limit = width // 4
    padded = -(-width // LANES) * LANES
    row_labels = lax.dynamic_slice_in_dim(vir_irrep, lax.axis_index("row") * row_block, row_block)
    col_labels = lax.dynamic_slice_in_dim(vir_irrep, lax.axis_index("col") * col_block, col_block)
    mixed = jnp.bitwise_xor(row_labels[:, None, None], col_labels[None, None, :])
    allowed = mixed == pair_irrep[None, :, None]
    sym_amp = jnp.where(allowed, amplitudes, jnp.zeros_like(amplitudes))
    piece = limit if col_block % limit == 0 else col_block
    folded = sym_amp[:, :, :piece]
    for start in range(piece, col_block, piece):
        folded = folded + sym_amp[:, :, start : start + piece]
    used = row_block * pairs_here * piece
    length = -(-(used + pairs_here) // (16 * LANES)) * 16 * LANES
    payload = jnp.concatenate([
        folded.reshape(-1), pair_irrep.astype(jnp.bfloat16),
        jnp.zeros((length - used - pairs_here,), jnp.bfloat16)])
    got = gather_all(sizes, count, payload.reshape(-1, LANES)).reshape(count, length)
    pis = got[:pgroups, used : used + pairs_here].astype(jnp.int32).reshape(-1)
    got = got[:, :used].reshape(rows, cols, pgroups, row_block, pairs_here, piece)
    got = jnp.transpose(got, (0, 3, 2, 4, 1, 5))
    got = got.reshape(width, pgroups * pairs_here, cols, 1, piece)
    got = jnp.broadcast_to(got, (width, pgroups * pairs_here, cols, col_block // piece, piece))
    got = got.reshape(width, pgroups * pairs_here, width)
    vir_mixed = jnp.bitwise_xor(vir_irrep[:, None], vir_irrep[None, :])
    t = jnp.where(vir_mixed[:, None, :] == pis[None, :, None], got, jnp.zeros_like(got))
    t = jnp.pad(t, ((0, 0), (0, 0), (0, padded - width)))
    t = t.reshape(width, pgroups * pairs_here * padded)
    packed = partial_ladder(factors, t, pis, vir_irrep, padded)
    packed = packed.reshape(pgroups * pairs_here, rows, row_block, LANES)
    mine = reduce_all(sizes, count, packed)
    spread = jnp.tile(jnp.swapaxes(mine, 0, 1), (1, 1, padded // LANES))
    spread = lax.dynamic_slice_in_dim(spread, lax.axis_index("col") * col_block, col_block, axis=2)
    return jnp.where(allowed, spread, jnp.zeros_like(spread))


def solution(mesh):
    placed = (P("row", "pair", "col"), P(("row", "col", "pair"), None, None), P(), P("pair"))
    return jax.shard_map(
        functools.partial(body, dict(mesh.shape)), mesh=mesh, in_specs=placed,
        out_specs=P("row", "pair", "col"), check_vma=False,
    )
```
